256 devices in a mesh: grp: 8 (over y, z_lo), dev: 32 (over x, z_hi, core).
Axes of the slice: x: 4, y: 4, z: 8 (z_hi: 4, z_lo: 2; z = z_hi * 2 + z_lo), core: 2. Of those that a mesh axis runs over, the one named last changes fastest.
Arguments:
- resp_q: bfloat16 [32768, 1024], P(('grp', 'dev')), may hold values from -256 to 256
- resp_k: bfloat16 [32768, 128], P(('grp', 'dev')), may hold values from -6 to 6
- resp_v: bfloat16 [32768, 128], P(('grp', 'dev')), may hold values from -6 to 6
- resp_out: bfloat16 [32768, 1024], P(('grp', 'dev')), may hold values from -6 to 6
- resp_grad: bfloat16 [32768, 1024], P(('grp', 'dev')), may hold values from -6 to 6
- prompt_k: bfloat16 [2048, 128], P('dev'), may hold values from -8 to 8
- prompt_v: bfloat16 [2048, 128], P('dev'), may hold values from -6 to 6
- lengths: int32 [8, 2], P('grp'), may hold values from 512 to 3584, as said below
Outputs:
- grad_q: bfloat16 [32768, 1024], P(('grp', 'dev'))
- grad_k: bfloat16 [32768, 128], P(('grp', 'dev'))
- grad_v: bfloat16 [32768, 128], P(('grp', 'dev'))
- prompt_grad_k: bfloat16 [2048, 128], P('dev')
- prompt_grad_v: bfloat16 [2048, 128], P('dev')
The draws below stay inside these ranges and needn't reach their ends.
Inputs may be any that keep to these rules, and one draw needn't show every extreme that they name: In every group the two lengths sum to 4096.
All inputs are finite; a program needn't handle non-finite values.
Results may differ from the reference program's by a relative error of at most 0.019.
Values may be sent and summed in bfloat16 or wider, within the bound.
No kernel may reach another device: no remote copies, remote signals or barrier semaphores. Data moves between devices by JAX's collectives and lax.ppermute only.
A program may use at most 128 MiB of HBM per device.

```python
import math
import jax
import jax.numpy as jnp
from jax import lax

HEAD_DIM = 128
Q_HEADS = 8
PROMPT = 2048
GROUP_ROWS = 4096
RESP_ROWS = 32768
N_GRP = 8


def shared_keys(key):
    return jax.random.normal(key, (PROMPT, HEAD_DIM), jnp.float32)


def draw_prompt_k(key, part):
    keys = shared_keys(key)
    return keys.astype(jnp.bfloat16)


def draw_resp_q(key, part):
    key = jax.random.fold_in(key, 7)
    values = jax.random.normal(key, (RESP_ROWS, Q_HEADS * HEAD_DIM), jnp.float32)
    return values.astype(jnp.bfloat16)


def draw_lengths(key, part):
    key = jax.random.fold_in(key, 5)
    lowest = GROUP_ROWS // 8
    leading = jax.random.randint(key, (N_GRP,), lowest, GROUP_ROWS - lowest + 1)
    leading = leading.at[0].set(lowest)
    return jnp.stack([leading, GROUP_ROWS - leading], axis=1).astype(jnp.int32)


def block_scale(rng, extent, cuts, low, high):
    gain, own = 1.0, jax.random.fold_in(rng, 6)
    for axis_at, parts in cuts:
        draws = jnp.exp(jax.random.uniform(jax.random.fold_in(own, axis_at), (parts,), jnp.float32, low / len(cuts), high / len(cuts)))
        gain = gain * jnp.repeat(draws, extent[axis_at] // parts).reshape([-1 if axis == axis_at else 1 for axis in range(len(extent))])
    return gain


def scatter_about(own_key, shape, deviation, reach, shards=(), kind=jnp.bfloat16):
    level = block_scale(own_key, shape, shards, -0.22, 0.18) if shards else 1.0
    values = jax.random.normal(own_key, shape, jnp.float32) * deviation * level
    return jnp.minimum(jnp.maximum(values, -reach), reach).astype(kind)


def setup_inputs(seed: int = 0) -> dict:
    arg_keys = jax.random.split(jax.random.key(seed), 9)
    resp_q = draw_resp_q(jax.random.fold_in(arg_keys[8], 71), 0)
    resp_k = scatter_about(arg_keys[1], (RESP_ROWS, HEAD_DIM), 1.0, 6.0, ((0, 256),))
    resp_v = scatter_about(arg_keys[2], (RESP_ROWS, HEAD_DIM), 1.0, 6.0, ((0, 256),))
    resp_out = scatter_about(arg_keys[3], (RESP_ROWS, Q_HEADS * HEAD_DIM), 1.0, 6.0, ((0, 256),))
    resp_grad = scatter_about(arg_keys[4], (RESP_ROWS, Q_HEADS * HEAD_DIM), 1.0, 6.0, ((0, 256),))
    prompt_k = draw_prompt_k(jax.random.fold_in(arg_keys[8], 71), 0)
    prompt_v = scatter_about(arg_keys[6], (PROMPT, HEAD_DIM), 1.0, 6.0, ((0, 32),))
    lengths = draw_lengths(jax.random.fold_in(arg_keys[8], 71), 0)
    return dict(resp_q=resp_q, resp_k=resp_k, resp_v=resp_v, resp_out=resp_out, resp_grad=resp_grad, prompt_k=prompt_k, prompt_v=prompt_v, lengths=lengths)


masked_score = -1e30


def block_grads(query, grad_rows, delta, keys, values, visible):
    scale = query.shape[2] ** -0.5
    query_wide = query.astype(jnp.float32)
    keys_wide = keys.astype(jnp.float32)
    grad_wide = grad_rows.astype(jnp.float32)
    scores = jnp.einsum("ihd,kd->hik", query_wide, keys_wide) * scale
    scores = jnp.where(visible[None], scores, masked_score)
    top = jnp.max(scores, axis=2)
    total = jnp.sum(jnp.where(visible[None], jnp.exp(scores - top[:, :, None]), 0.0), axis=2)
    log_total = top + jnp.log(total)
    probs = jnp.where(visible[None], jnp.exp(scores - log_total[:, :, None]), 0.0)
    probs_low = lax.optimization_barrier(probs.astype(jnp.bfloat16)).astype(jnp.float32)
    grad_values = jnp.einsum("hik,ihd->kd", probs_low, grad_wide)
    grad_probs = jnp.einsum("ihd,kd->hik", grad_wide, values.astype(jnp.float32))
    grad_scores = (probs * (grad_probs - delta[:, :, None])).astype(jnp.bfloat16)
    grad_scores = lax.optimization_barrier(grad_scores).astype(jnp.float32)
    grad_query = jnp.einsum("hik,kd->ihd", grad_scores, keys_wide) * scale
    grad_keys = jnp.einsum("hik,ihd->kd", grad_scores, query_wide) * scale
    return grad_query, grad_keys, grad_values


def reference(resp_q, resp_k, resp_v, resp_out, resp_grad, prompt_k, prompt_v, lengths):
    groups = lengths.shape[0]
    group_rows = resp_k.shape[0] // groups
    prompt_rows = prompt_k.shape[0]
    head = resp_k.shape[1]
    heads = resp_q.shape[1] // head
    block = math.gcd(group_rows, 512)
    blocks = group_rows // block
    query_all = resp_q.reshape(groups, blocks, block, heads, head)
    grad_all = resp_grad.reshape(groups, blocks, block, heads, head)
    output_all = resp_out.reshape(groups, blocks, block, heads, head)
    keys_all = resp_k.reshape(groups, group_rows, head)
    values_all = resp_v.reshape(groups, group_rows, head)

    def per_group(carry, inputs):
        prompt_keys_sum, prompt_values_sum = carry
        queries, grads, outputs, group_keys, group_values, split = inputs
        keys = jnp.concatenate([prompt_k, group_keys], 0)
        values = jnp.concatenate([prompt_v, group_values], 0)
        key_ids = jnp.arange(group_rows, dtype=jnp.int32)
        key_part = key_ids >= split

        def per_block(inner, block_inputs):
            keys_sum, values_sum = inner
            index, query, grad_rows, output_rows = block_inputs
            row_ids = index * block + jnp.arange(block, dtype=jnp.int32)
            own_part = row_ids >= split
            visible_resp = (key_part[None, :] == own_part[:, None]) & (key_ids[None, :] <= row_ids[:, None])
            visible = jnp.concatenate([jnp.ones((block, prompt_rows), bool), visible_resp], 1)
            delta = jnp.sum(grad_rows.astype(jnp.float32) * output_rows.astype(jnp.float32), axis=2).T
            grad_query, grad_keys, grad_values = block_grads(query, grad_rows, delta, keys, values, visible)
            return (keys_sum + grad_keys, values_sum + grad_values), grad_query

        start_sums = jnp.zeros((prompt_rows + group_rows, head), jnp.float32)
        block_ids = jnp.arange(blocks, dtype=jnp.int32)
        (keys_sum, values_sum), grad_query = lax.scan(per_block, (start_sums, start_sums), (block_ids, queries, grads, outputs))
        carry = (prompt_keys_sum + keys_sum[:prompt_rows], prompt_values_sum + values_sum[:prompt_rows])
        return carry, (grad_query, keys_sum[prompt_rows:], values_sum[prompt_rows:])

    start_prompt = jnp.zeros((prompt_rows, head), jnp.float32)
    (prompt_keys_sum, prompt_values_sum), (grad_query, grad_keys, grad_values) = lax.scan(
        per_group, (start_prompt, start_prompt), (query_all, grad_all, output_all, keys_all, values_all, lengths[:, 0]))
    return (grad_query.reshape(groups * group_rows, heads * head).astype(jnp.bfloat16),
            grad_keys.reshape(groups * group_rows, head).astype(jnp.bfloat16),
            grad_values.reshape(groups * group_rows, head).astype(jnp.bfloat16),
            prompt_keys_sum.astype(jnp.bfloat16),
            prompt_values_sum.astype(jnp.bfloat16))
```

```python
import functools
import math

import jax
import jax.numpy as jnp
from jax import lax
from jax.experimental import pallas as pl
from jax.experimental.pallas import tpu as pltpu
from jax.sharding import PartitionSpec as P

X, Z, C = 4, 4, 2
STEPS = (0, 1, 3, 2)
DEV = [(x, z, c) for x in range(X) for z in range(Z) for c in range(C)]
lowest = -1e30
f32, bf16 = jnp.float32, jnp.bfloat16
NT = (((1,), (1,)), ((), ()))
NN = (((1,), (0,)), ((), ()))
TN = (((0,), (0,)), ((), ()))


def dot(a, b, dims):
    return lax.dot_general(a, b, dims, preferred_element_type=f32)


def number(x, z, c):
    return ((x % X) * Z + z % Z) * C + c % C


def swap_core(a):
    return lax.ppermute(a, "dev", [(number(x, z, c), number(x, z, c + 1)) for x, z, c in DEV])


def shift_x(a, step):
    return lax.ppermute(a, "dev", [(number(x, z, c), number(x + step, z, c)) for x, z, c in DEV])


def shift_z(a, step):
    return lax.ppermute(a, "dev", [(number(x, z, c), number(x, z + step, c)) for x, z, c in DEV])


def shift_y(a, step):
    return lax.ppermute(a, "grp", [(y * 2 + l, (y + step) % 4 * 2 + l) for y in range(4) for l in range(2)])


def swap_pair(a):
    return lax.ppermute(a, "grp", [(y * 2 + l, y * 2 + 1 - l) for y in range(4) for l in range(2)])


def gather(shift, a):
    return [a] + [shift(a, step) for step in STEPS[1:]]


def scatter_sum(shift, parts):
    total = parts[0].astype(f32)
    for step, part in zip(STEPS[1:], parts[1:]):
        total = total + shift(part, -step).astype(f32)
    return total


def row_ids(info, rows):
    place = lax.broadcasted_iota(jnp.int32, (1, C * rows), 1)
    core = jnp.where(place < rows, info[2], 1 - info[2])
    return (info[0] * Z + info[1]) * (C * rows) + core * rows + place % rows


def key_ids(info, back, rows):
    place = lax.broadcasted_iota(jnp.int32, (Z * rows, 1), 0)
    x = lax.rem(info[0] + (X - back), X)
    ids = jnp.zeros((Z * rows, 1), jnp.int32)
    for r, step in enumerate(STEPS):
        z = lax.rem(info[1] + (Z - step), Z)
        ids = jnp.where(place // rows == r, (x * Z + z) * (C * rows) + info[2] * rows + place % rows, ids)
    return ids


def seen(info, back, rows):
    x = lax.rem(info[0] + (X - back), X)
    split = info[3]
    first = x * (Z * C * rows)
    row = (info[0] * Z + info[1]) * (C * rows)
    return (x <= info[0]) & ((row < split) | (first + Z * C * rows > split))


def mask_of(info, back, rows):
    t = row_ids(info, rows)
    u = key_ids(info, back, rows)
    start = jnp.where(t >= info[3], info[3], 0)
    return (u <= t) & (u >= start)


def stats_kernel(heads, rows, c, info, q_own, q_other, grad_own, out_own, k0, k1, k2, k3, st):
    head = 128
    keys = (k0, k1, k2, k3)
    resp = Z * rows
    q = jnp.concatenate([q_own[...], q_other[...]], axis=0)
    st[0:heads, :] = jnp.full((heads, C * rows), lowest, f32)
    st[heads:2 * heads, :] = jnp.zeros((heads, C * rows), f32)
    prod = grad_own[...].astype(f32) * out_own[...].astype(f32)
    for h in range(heads):
        delta = jnp.sum(prod[:, h * head:(h + 1) * head].T, axis=0, keepdims=True)
        st[2 * heads + h:2 * heads + h + 1, :] = jnp.concatenate([delta, delta], axis=1)

    def step(k, mask):
        for h in range(heads):
            s = dot(k, q[:, h * head:(h + 1) * head], NT) * c
            if mask is not None:
                s = jnp.where(mask, s, lowest)
            old = st[h:h + 1, :]
            new = jnp.maximum(old, jnp.max(s, axis=0, keepdims=True))
            total = jnp.sum(jnp.exp2(s - new), axis=0, keepdims=True)
            st[h:h + 1, :] = new
            st[heads + h:heads + h + 1, :] = st[heads + h:heads + h + 1, :] * jnp.exp2(old - new) + total

    for r in range(X):
        step(keys[r][resp:, :], None)
    for r, back in enumerate(STEPS):
        @pl.when(seen(info, back, rows))
        def _():
            step(keys[r][:resp, :], mask_of(info, back, rows))


def combine(heads, rows, st, st_other):
    def turned(a):
        return jnp.concatenate([a[:, rows:], a[:, :rows]], axis=1)
    top, top_other = st[0:heads, :], turned(st_other[0:heads, :])
    total, total_other = st[heads:2 * heads, :], turned(st_other[heads:2 * heads, :])
    m = jnp.maximum(top, top_other)
    lse = m + jnp.log2(total * jnp.exp2(top - m) + total_other * jnp.exp2(top_other - m))
    delta = jnp.concatenate([st[2 * heads:, 0:rows], st_other[2 * heads:, 0:rows]], axis=1)
    return lse, delta


def grads_step(heads, rows, c, k, v, q, grad, lse, delta, mask, dq, dkv):
    head = 128
    scale = head ** -0.5
    dk = jnp.zeros(k.shape, f32)
    dv = jnp.zeros(v.shape, f32)
    for h in range(heads):
        cols = slice(h * head, (h + 1) * head)
        s = dot(k, q[:, cols], NT) * c
        p = jnp.exp2(s - lse[h:h + 1, :])
        if mask is not None:
            p = jnp.where(mask, p, 0.0)
        ds = (p * (dot(v, grad[:, cols], NT) - delta[h:h + 1, :])).astype(bf16)
        dv = dv + dot(p.astype(bf16), grad[:, cols], NN)
        dk = dk + dot(ds, q[:, cols], NN)
        dq[:, cols] += dot(ds, k, TN)
    dkv[:, 0:head] = (dk * scale).astype(bf16)
    dkv[:, head:] = dv.astype(bf16)


def prompt_kernel(heads, rows, c, info, st, st_other, q_own, q_other, grad_own, grad_other,
                  k0, k1, k2, k3, v0, v1, v2, v3, o0, o1, o2, o3, dq):
    resp = Z * rows
    q = jnp.concatenate([q_own[...], q_other[...]], axis=0)
    grad = jnp.concatenate([grad_own[...], grad_other[...]], axis=0)
    lse, delta = combine(heads, rows, st, st_other)
    dq[...] = jnp.zeros(dq.shape, f32)
    for k, v, o in zip((k0, k1, k2, k3), (v0, v1, v2, v3), (o0, o1, o2, o3)):
        grads_step(heads, rows, c, k[resp:, :], v[resp:, :], q, grad, lse, delta, None, dq, o)


def resp_kernel(heads, rows, c, info, st, st_other, q_own, q_other, grad_own, grad_other,
                k0, k1, k2, k3, v0, v1, v2, v3, dq_in, o0, o1, o2, o3, dq_own, dq_other, dq):
    resp = Z * rows
    scale = 128 ** -0.5
    q = jnp.concatenate([q_own[...], q_other[...]], axis=0)
    grad = jnp.concatenate([grad_own[...], grad_other[...]], axis=0)
    lse, delta = combine(heads, rows, st, st_other)
    dq[...] = dq_in[...]
    for k, v, o, back in zip((k0, k1, k2, k3), (v0, v1, v2, v3), (o0, o1, o2, o3), STEPS):
        visible = seen(info, back, rows)

        @pl.when(visible)
        def _():
            mask = mask_of(info, back, rows)
            grads_step(heads, rows, c, k[:resp, :], v[:resp, :], q, grad, lse, delta, mask, dq, o)

        @pl.when(jnp.logical_not(visible))
        def _():
            o[...] = jnp.zeros(o.shape, o.dtype)
    dq_own[...] = dq[0:rows, :] * scale
    dq_other[...] = dq[rows:, :] * scale


def call(kernel, out_shapes, args, flops, scratch=()):
    smem, vmem = pl.BlockSpec(memory_space=pltpu.SMEM), pl.BlockSpec(memory_space=pltpu.VMEM)
    size = sum(a.size * a.dtype.itemsize for a in args)
    return pl.pallas_call(
        kernel,
        out_shape=out_shapes,
        in_specs=[smem] + [vmem] * (len(args) - 1),
        out_specs=[vmem] * len(out_shapes),
        scratch_shapes=list(scratch),
        compiler_params=pltpu.CompilerParams(vmem_limit_bytes=48 * 1024 * 1024),
        cost_estimate=pl.CostEstimate(flops=flops, bytes_accessed=size, transcendentals=0),
    )(*args)


def on_device(resp_q, resp_k, resp_v, resp_out, resp_grad, prompt_k, prompt_v, lengths):
    rows, width = resp_q.shape
    head = resp_k.shape[1]
    heads = width // head
    prompt = prompt_k.shape[0]
    c = head ** -0.5 * math.log2(math.e)
    resp_keys, prompt_keys = Z * rows, Z * prompt
    me = lax.axis_index("dev")
    info = jnp.stack([me // (Z * C), me // C % Z, me % C, lengths[0, 0]]).astype(jnp.int32)
    shape = jax.ShapeDtypeStruct

    def along_z(resp, shared):
        blocks = gather(shift_z, jnp.concatenate([resp, shared], axis=0))
        return jnp.concatenate([b[:rows] for b in blocks] + [b[rows:] for b in blocks], axis=0)

    k_column = along_z(resp_k, prompt_k)
    v_column = along_z(resp_v, prompt_v)
    q_other, grad_other = swap_core(resp_q), swap_core(resp_grad)
    k_all = gather(shift_x, k_column)
    v_all = gather(shift_x, v_column)

    flops = 2 * C * rows * heads * head * X
    st, = call(
        functools.partial(stats_kernel, heads, rows, c),
        [shape((3 * heads, C * rows), f32)],
        [info, resp_q, q_other, resp_grad, resp_out, *k_all],
        flops * (resp_keys + prompt_keys),
    )
    st_other = swap_core(st)
    common = [info, st, st_other, resp_q, q_other, resp_grad, grad_other, *k_all, *v_all]
    *prompt_parts, dq = call(
        functools.partial(prompt_kernel, heads, rows, c),
        [shape((prompt_keys, 2 * head), bf16)] * X + [shape((C * rows, width), f32)],
        common,
        5 * flops * prompt_keys,
    )
    *resp_parts, dq_own, dq_other = call(
        functools.partial(resp_kernel, heads, rows, c),
        [shape((resp_keys, 2 * head), bf16)] * X + [shape((rows, width), f32)] * 2,
        common + [dq],
        5 * flops * resp_keys,
        [pltpu.VMEM((C * rows, width), f32)],
    )

    def reduced(parts, size):
        column = scatter_sum(shift_x, parts).astype(bf16)
        return scatter_sum(shift_z, [column[r * size:(r + 1) * size] for r in range(Z)])

    own_prompt = reduced(prompt_parts, prompt)
    own_prompt = own_prompt + swap_pair(own_prompt)
    own_prompt = (own_prompt + shift_y(own_prompt, 2)) + (shift_y(own_prompt, 1) + shift_y(own_prompt, 3))
    own_resp = reduced(resp_parts, rows)
    grad_q = dq_own + swap_core(dq_other)
    return (
        grad_q.astype(bf16),
        own_resp[:, :head].astype(bf16),
        own_resp[:, head:].astype(bf16),
        own_prompt[:, :head].astype(bf16),
        own_prompt[:, head:].astype(bf16),
    )


def solution(mesh):
    rows, shared, group = P(("grp", "dev"), None), P("dev", None), P("grp", None)
    return jax.shard_map(
        on_device,
        mesh=mesh,
        in_specs=(rows, rows, rows, rows, rows, shared, shared, group),
        out_specs=(rows, rows, rows, shared, shared),
        check_vma=False,
    )
```

```python
import functools
import math

import jax
import jax.numpy as jnp
from jax import lax
from jax.experimental import pallas as pl
from jax.experimental.pallas import tpu as pltpu
from jax.sharding import PartitionSpec as P

X, Z, C = 4, 4, 2
STEPS = (0, 1, 3, 2)
DEV = [(x, z, c) for x in range(X) for z in range(Z) for c in range(C)]
lowest = -1e30
f32, bf16 = jnp.float32, jnp.bfloat16
NT = (((1,), (1,)), ((), ()))
NN = (((1,), (0,)), ((), ()))
TN = (((0,), (0,)), ((), ()))


def dot(a, b, dims):
    return lax.dot_general(a, b, dims, preferred_element_type=f32)


def number(x, z, c):
    return ((x % X) * Z + z % Z) * C + c % C


def swap_core(a):
    return lax.ppermute(a, "dev", [(number(x, z, c), number(x, z, c + 1)) for x, z, c in DEV])


def shift_x(a, step):
    return lax.ppermute(a, "dev", [(number(x, z, c), number(x + step, z, c)) for x, z, c in DEV])


def shift_z(a, step):
    return lax.ppermute(a, "dev", [(number(x, z, c), number(x, z + step, c)) for x, z, c in DEV])


def shift_y(a, step):
    return lax.ppermute(a, "grp", [(y * 2 + l, (y + step) % 4 * 2 + l) for y in range(4) for l in range(2)])


def swap_pair(a):
    return lax.ppermute(a, "grp", [(y * 2 + l, y * 2 + 1 - l) for y in range(4) for l in range(2)])


def gather(shift, a):
    return [a] + [shift(a, step) for step in STEPS[1:]]


def scatter_sum(shift, parts):
    total = parts[0].astype(f32)
    for step, part in zip(STEPS[1:], parts[1:]):
        total = total + shift(part, -step).astype(f32)
    return total


def row_ids(info, rows):
    place = lax.broadcasted_iota(jnp.int32, (1, C * rows), 1)
    core = jnp.where(place < rows, info[2], 1 - info[2])
    return (info[0] * Z + info[1]) * (C * rows) + core * rows + place % rows


def key_ids(info, back, rows):
    place = lax.broadcasted_iota(jnp.int32, (Z * rows, 1), 0)
    x = lax.rem(info[0] + (X - back), X)
    ids = jnp.zeros((Z * rows, 1), jnp.int32)
    for r, step in enumerate(STEPS):
        z = lax.rem(info[1] + (Z - step), Z)
        ids = jnp.where(place // rows == r, (x * Z + z) * (C * rows) + info[2] * rows + place % rows, ids)
    return ids


def seen(info, back, rows):
    x = lax.rem(info[0] + (X - back), X)
    split = info[3]
    first = x * (Z * C * rows)
    row = (info[0] * Z + info[1]) * (C * rows)
    return (x <= info[0]) & ((row < split) | (first + Z * C * rows > split))


def mask_of(info, back, rows):
    t = row_ids(info, rows)
    u = key_ids(info, back, rows)
    mask = u >= jnp.where(t >= info[3], info[3], 0)
    return mask & (u <= t) if back == 0 else mask


def masked(a, mask, fill):
    if mask is None:
        return a
    n = mask.shape[0]
    return jnp.concatenate([jnp.where(mask, a[:n], fill), a[n:]], axis=0)


def stats_step(heads, c, k, q_own, q_other, mask, st):
    head = 128
    for h in range(heads):
        cols = slice(h * head, (h + 1) * head)
        q = jnp.concatenate([q_own[:, cols], q_other[:, cols]], axis=0)
        s = masked(dot(k, q, NT) * c, mask, lowest)
        old = st[h:h + 1, :]
        new = jnp.maximum(old, jnp.max(s, axis=0, keepdims=True))
        total = jnp.sum(jnp.exp2(s - new), axis=0, keepdims=True)
        st[h:h + 1, :] = new
        st[heads + h:heads + h + 1, :] = st[heads + h:heads + h + 1, :] * jnp.exp2(old - new) + total


def first_stats_kernel(heads, rows, c, info, q_own, q_other, grad_own, out_own, k0, st):
    head = 128
    st[0:heads, :] = jnp.full((heads, C * rows), lowest, f32)
    st[heads:2 * heads, :] = jnp.zeros((heads, C * rows), f32)
    prod = grad_own[...].astype(f32) * out_own[...].astype(f32)
    for h in range(heads):
        delta = jnp.sum(prod[:, h * head:(h + 1) * head].T, axis=0, keepdims=True)
        st[2 * heads + h:2 * heads + h + 1, :] = jnp.concatenate([delta, delta], axis=1)
    stats_step(heads, c, k0[...], q_own, q_other, mask_of(info, 0, rows), st)


def stats_kernel(heads, rows, c, info, st_in, q_own, q_other, k1, k2, k3, st):
    st[...] = st_in[...]
    for k, back in zip((k1, k2, k3), STEPS[1:]):
        visible = seen(info, back, rows)

        @pl.when(visible)
        def _():
            stats_step(heads, c, k[...], q_own, q_other, mask_of(info, back, rows), st)

        @pl.when(jnp.logical_not(visible))
        def _():
            stats_step(heads, c, k[Z * rows:, :], q_own, q_other, None, st)


def combine(heads, rows, st, st_other):
    def turned(a):
        return jnp.concatenate([a[:, rows:], a[:, :rows]], axis=1)
    top, top_other = st[0:heads, :], turned(st_other[0:heads, :])
    total, total_other = st[heads:2 * heads, :], turned(st_other[heads:2 * heads, :])
    m = jnp.maximum(top, top_other)
    lse = m + jnp.log2(total * jnp.exp2(top - m) + total_other * jnp.exp2(top_other - m))
    delta = jnp.concatenate([st[2 * heads:, 0:rows], st_other[2 * heads:, 0:rows]], axis=1)
    return lse, delta


def grads_step(heads, c, k, v, q, grad, lse, delta, mask, p_all, ds_all, dq, dkv):
    head = 128
    wide = lse.shape[1]
    n = k.shape[0]
    for h in range(heads):
        at = slice(h * wide, (h + 1) * wide)
        p = masked(jnp.exp2(dot(k, q[at, :], NT) * c - lse[h:h + 1, :]), mask, 0.0)
        p_all[0:n, at] = p.astype(bf16)
        ds_all[0:n, at] = (p * (dot(v, grad[at, :], NT) - delta[h:h + 1, :])).astype(bf16)
    dq[...] += dot(k.T, ds_all[0:n, :], NN)
    dv = dot(p_all[0:n, :], grad[...], NN)
    dk = dot(ds_all[0:n, :], q[...], NN) * head ** -0.5
    return jnp.concatenate([dk, dv], axis=1)


def grads_kernel(heads, rows, c, back, first, last, info, st, st_other, q_own, q_other, grad_own, grad_other, k, v, *refs):
    head = 128
    wide = C * rows
    resp = Z * rows
    refs = list(refs)
    dq_in = None if first else refs.pop(0)
    arrived = refs.pop(0) if last else None
    dkv = refs.pop(0)
    dq_out = [refs.pop(0), refs.pop(0)] if last else [refs.pop(0)]
    q, grad, p_all, ds_all = refs[:4]
    dq = refs[4] if last else dq_out[0]
    for h in range(heads):
        cols = slice(h * head, (h + 1) * head)
        for i, (a, b) in enumerate(((q_own, grad_own), (q_other, grad_other))):
            at = slice(h * wide + i * rows, h * wide + (i + 1) * rows)
            q[at, :] = a[:, cols]
            grad[at, :] = b[:, cols]
    lse, delta = combine(heads, rows, st, st_other)
    dq[...] = jnp.zeros(dq.shape, f32) if first else dq_in[...]

    def step(a, mask):
        return grads_step(heads, c, k[a:, :], v[a:, :], q, grad, lse, delta, mask, p_all, ds_all, dq, dkv)

    if back == 0:
        dkv[...] = arrived[...].astype(f32) + step(0, mask_of(info, back, rows))
    else:
        visible = seen(info, back, rows)

        @pl.when(visible)
        def _():
            dkv[...] = step(0, mask_of(info, back, rows)).astype(bf16)

        @pl.when(jnp.logical_not(visible))
        def _():
            dkv[0:resp, :] = jnp.zeros((resp, 2 * head), bf16)
            dkv[resp:, :] = step(resp, None).astype(bf16)
    if last:
        for h in range(heads):
            part = dq[:, h * wide:(h + 1) * wide].T * head ** -0.5
            dq_out[0][:, h * head:(h + 1) * head] = part[0:rows, :]
            dq_out[1][:, h * head:(h + 1) * head] = part[rows:, :]


def call(kernel, out_shapes, args, flops, scratch=()):
    smem, vmem = pl.BlockSpec(memory_space=pltpu.SMEM), pl.BlockSpec(memory_space=pltpu.VMEM)
    size = sum(a.size * a.dtype.itemsize for a in args)
    return pl.pallas_call(
        kernel,
        out_shape=out_shapes,
        in_specs=[smem] + [vmem] * (len(args) - 1),
        out_specs=[vmem] * len(out_shapes),
        scratch_shapes=list(scratch),
        compiler_params=pltpu.CompilerParams(vmem_limit_bytes=48 * 1024 * 1024),
        cost_estimate=pl.CostEstimate(flops=flops, bytes_accessed=size, transcendentals=0),
    )(*args)


def on_device(resp_q, resp_k, resp_v, resp_out, resp_grad, prompt_k, prompt_v, lengths):
    rows, width = resp_q.shape
    head = resp_k.shape[1]
    heads = width // head
    prompt = prompt_k.shape[0]
    c = head ** -0.5 * math.log2(math.e)
    resp_keys, prompt_keys = Z * rows, Z * prompt
    me = lax.axis_index("dev")
    info = jnp.stack([me // (Z * C), me // C % Z, me % C, lengths[0, 0]]).astype(jnp.int32)
    shape = jax.ShapeDtypeStruct

    q_other = swap_core(resp_q)
    pairs = jnp.concatenate(
        [jnp.concatenate([resp_k, resp_v], axis=1), jnp.concatenate([prompt_k, prompt_v], axis=1)], axis=0
    )
    blocks = gather(shift_z, pairs)
    column = jnp.concatenate([b[:rows] for b in blocks] + [b[rows:] for b in blocks], axis=0)
    k_all = gather(shift_x, column[:, :head])
    v_all = gather(shift_x, column[:, head:])
    grad_other = swap_core(resp_grad)

    keys = resp_keys + prompt_keys
    flops = 2 * C * rows * heads * head * keys
    st_shape = shape((3 * heads, C * rows), f32)
    st, = call(
        functools.partial(first_stats_kernel, heads, rows, c),
        [st_shape], [info, resp_q, q_other, resp_grad, resp_out, k_all[0]], flops,
    )
    st, = call(
        functools.partial(stats_kernel, heads, rows, c),
        [st_shape], [info, st, resp_q, q_other, *k_all[1:]], flops * 3,
    )
    st_other = swap_core(st)
    arrived, dq = [], []
    for i, r in enumerate((3, 1, 2, 0)):
        first, last = i == 0, i == X - 1
        out = [shape((keys, 2 * head), f32 if last else bf16)]
        out += [shape((rows, width), f32)] * 2 if last else [shape((head, C * rows * heads), f32)]
        scratch = [pltpu.VMEM((C * rows * heads, head), bf16)] * 2 + [pltpu.VMEM((keys, C * rows * heads), bf16)] * 2
        if last:
            scratch.append(pltpu.VMEM((head, C * rows * heads), f32))
        part, *dq = call(
            functools.partial(grads_kernel, heads, rows, c, STEPS[r], first, last),
            out,
            [info, st, st_other, resp_q, q_other, resp_grad, grad_other, k_all[r], v_all[r]]
            + dq + (arrived[:1] if last else []),
            5 * flops,
            scratch,
        )
        if not last:
            arrived.append(shift_x(part, -STEPS[r]))
    dq_own, dq_other = dq

    mine = (part + (arrived[1].astype(f32) + arrived[2].astype(f32))).astype(bf16)
    mine = [
        jnp.concatenate(
            [mine[r * rows:(r + 1) * rows], mine[resp_keys + r * prompt:resp_keys + (r + 1) * prompt]], axis=0
        )
        for r in range(Z)
    ]
    own = scatter_sum(shift_z, mine)
    own_resp, own_prompt = own[:rows], own[rows:]
    own_prompt = own_prompt + swap_pair(own_prompt)
    own_prompt = (own_prompt + shift_y(own_prompt, 2)) + (shift_y(own_prompt, 1) + shift_y(own_prompt, 3))
    grad_q = dq_own + swap_core(dq_other)
    return (
        grad_q.astype(bf16),
        own_resp[:, :head].astype(bf16),
        own_resp[:, head:].astype(bf16),
        own_prompt[:, :head].astype(bf16),
        own_prompt[:, head:].astype(bf16),
    )


def solution(mesh):
    rows, shared, group = P(("grp", "dev"), None), P("dev", None), P("grp", None)
    return jax.shard_map(
        on_device,
        mesh=mesh,
        in_specs=(rows, rows, rows, rows, rows, shared, shared, group),
        out_specs=(rows, rows, rows, shared, shared),
        check_vma=False,
    )
```

```python
import functools
import math

import jax
import jax.numpy as jnp
from jax import lax
from jax.experimental import pallas as pl
from jax.experimental.pallas import tpu as pltpu
from jax.sharding import PartitionSpec as P

X, Z, C = 4, 4, 2
STEPS = (0, 1, 3, 2)
DEV = [(x, z, c) for x in range(X) for z in range(Z) for c in range(C)]
lowest = -1e30
f32, bf16 = jnp.float32, jnp.bfloat16
NT = (((1,), (1,)), ((), ()))
NN = (((1,), (0,)), ((), ()))
TN = (((0,), (0,)), ((), ()))


def dot(a, b, dims):
    return lax.dot_general(a, b, dims, preferred_element_type=f32)


def number(x, z, c):
    return ((x % X) * Z + z % Z) * C + c % C


def swap_core(a):
    return lax.ppermute(a, "dev", [(number(x, z, c), number(x, z, c + 1)) for x, z, c in DEV])


def shift_x(a, step):
    return lax.ppermute(a, "dev", [(number(x, z, c), number(x + step, z, c)) for x, z, c in DEV])


def shift_z(a, step):
    return lax.ppermute(a, "dev", [(number(x, z, c), number(x, z + step, c)) for x, z, c in DEV])


def shift_y(a, step):
    return lax.ppermute(a, "grp", [(y * 2 + l, (y + step) % 4 * 2 + l) for y in range(4) for l in range(2)])


def swap_pair(a):
    return lax.ppermute(a, "grp", [(y * 2 + l, y * 2 + 1 - l) for y in range(4) for l in range(2)])


def gather(shift, a):
    return [a] + [shift(a, step) for step in STEPS[1:]]


def scatter_sum(shift, parts):
    total = parts[0].astype(f32)
    for step, part in zip(STEPS[1:], parts[1:]):
        total = total + shift(part, -step).astype(f32)
    return total


def row_ids(info, rows):
    place = lax.broadcasted_iota(jnp.int32, (1, C * rows), 1)
    core = jnp.where(place < rows, info[2], 1 - info[2])
    return (info[0] * Z + info[1]) * (C * rows) + core * rows + place % rows


def key_ids(info, back, rows):
    place = lax.broadcasted_iota(jnp.int32, (Z * rows, 1), 0)
    x = lax.rem(info[0] + (X - back), X)
    ids = jnp.zeros((Z * rows, 1), jnp.int32)
    for r, step in enumerate(STEPS):
        z = lax.rem(info[1] + (Z - step), Z)
        ids = jnp.where(place // rows == r, (x * Z + z) * (C * rows) + info[2] * rows + place % rows, ids)
    return ids


def seen(info, back, rows):
    x = lax.rem(info[0] + (X - back), X)
    split = info[3]
    first = x * (Z * C * rows)
    row = (info[0] * Z + info[1]) * (C * rows)
    return (x <= info[0]) & ((row < split) | (first + Z * C * rows > split))


def mask_of(info, back, rows):
    t = row_ids(info, rows)
    u = key_ids(info, back, rows)
    mask = u >= jnp.where(t >= info[3], info[3], 0)
    return mask & (u <= t) if back == 0 else mask


def masked(a, mask, fill):
    if mask is None:
        return a
    n = mask.shape[0]
    return jnp.concatenate([jnp.where(mask, a[:n], fill), a[n:]], axis=0)


def stats_step(heads, c, k, q_own, q_other, mask, st):
    head = 128
    for h in range(heads):
        cols = slice(h * head, (h + 1) * head)
        q = jnp.concatenate([q_own[:, cols], q_other[:, cols]], axis=0)
        s = masked(dot(k, q, NT) * c, mask, lowest)
        old = st[h:h + 1, :]
        new = jnp.maximum(old, jnp.max(s, axis=0, keepdims=True))
        total = jnp.sum(jnp.exp2(s - new), axis=0, keepdims=True)
        st[h:h + 1, :] = new
        st[heads + h:heads + h + 1, :] = st[heads + h:heads + h + 1, :] * jnp.exp2(old - new) + total


def first_stats_kernel(heads, rows, c, info, q_own, q_other, grad_own, out_own, k0, st):
    head = 128
    st[0:heads, :] = jnp.full((heads, C * rows), lowest, f32)
    st[heads:2 * heads, :] = jnp.zeros((heads, C * rows), f32)
    prod = grad_own[...].astype(f32) * out_own[...].astype(f32)
    for h in range(heads):
        delta = jnp.sum(prod[:, h * head:(h + 1) * head].T, axis=0, keepdims=True)
        st[2 * heads + h:2 * heads + h + 1, :] = jnp.concatenate([delta, delta], axis=1)
    stats_step(heads, c, k0[...], q_own, q_other, mask_of(info, 0, rows), st)


def stats_kernel(heads, rows, c, info, st_in, q_own, q_other, k1, k2, k3, st):
    st[...] = st_in[...]
    for k, back in zip((k1, k2, k3), STEPS[1:]):
        visible = seen(info, back, rows)

        @pl.when(visible)
        def _():
            stats_step(heads, c, k[...], q_own, q_other, mask_of(info, back, rows), st)

        @pl.when(jnp.logical_not(visible))
        def _():
            stats_step(heads, c, k[Z * rows:, :], q_own, q_other, None, st)


def combine(heads, rows, st, st_other):
    def turned(a):
        return jnp.concatenate([a[:, rows:], a[:, :rows]], axis=1)
    top, top_other = st[0:heads, :], turned(st_other[0:heads, :])
    total, total_other = st[heads:2 * heads, :], turned(st_other[heads:2 * heads, :])
    m = jnp.maximum(top, top_other)
    lse = m + jnp.log2(total * jnp.exp2(top - m) + total_other * jnp.exp2(top_other - m))
    delta = jnp.concatenate([st[2 * heads:, 0:rows], st_other[2 * heads:, 0:rows]], axis=1)
    return lse, delta


def grads_step(heads, c, k, v, q, grad, lse, delta, mask, p_all, ds_all, dq, dkv):
    head = 128
    wide = lse.shape[1]
    n = k.shape[0]
    for h in range(heads):
        at = slice(h * wide, (h + 1) * wide)
        p = masked(jnp.exp2(dot(k, q[at, :], NT) * c - lse[h:h + 1, :]), mask, 0.0)
        p_all[0:n, at] = p.astype(bf16)
        ds_all[0:n, at] = (p * (dot(v, grad[at, :], NT) - delta[h:h + 1, :])).astype(bf16)
    dq[...] += dot(k.T, ds_all[0:n, :], NN)
    dv = dot(p_all[0:n, :], grad[...], NN)
    dk = dot(ds_all[0:n, :], q[...], NN) * head ** -0.5
    return jnp.concatenate([dk, dv], axis=1)


def grads_kernel(heads, rows, c, back, first, last, info, st, st_other, q_own, q_other, grad_own, grad_other, k, v, *refs):
    head = 128
    wide = C * rows
    resp = Z * rows
    refs = list(refs)
    dq_in = None if first else refs.pop(0)
    arrived = refs.pop(0) if last else None
    dkv = refs.pop(0)
    dq_out = [refs.pop(0), refs.pop(0)] if last else [refs.pop(0)]
    q, grad, p_all, ds_all = refs[:4]
    dq = refs[4] if last else dq_out[0]
    for h in range(heads):
        cols = slice(h * head, (h + 1) * head)
        for i, (a, b) in enumerate(((q_own, grad_own), (q_other, grad_other))):
            at = slice(h * wide + i * rows, h * wide + (i + 1) * rows)
            q[at, :] = a[:, cols]
            grad[at, :] = b[:, cols]
    lse, delta = combine(heads, rows, st, st_other)
    dq[...] = jnp.zeros(dq.shape, f32) if first else dq_in[...]

    def step(a, mask):
        return grads_step(heads, c, k[a:, :], v[a:, :], q, grad, lse, delta, mask, p_all, ds_all, dq, dkv)

    if back == 0:
        dkv[...] = arrived[...].astype(f32) + step(0, mask_of(info, back, rows))
    else:
        visible = seen(info, back, rows)

        @pl.when(visible)
        def _():
            dkv[...] = step(0, mask_of(info, back, rows)).astype(bf16)

        @pl.when(jnp.logical_not(visible))
        def _():
            dkv[0:resp, :] = jnp.zeros((resp, 2 * head), bf16)
            dkv[resp:, :] = step(resp, None).astype(bf16)
    if last:
        for h in range(heads):
            part = dq[:, h * wide:(h + 1) * wide].T * head ** -0.5
            dq_out[0][:, h * head:(h + 1) * head] = part[0:rows, :]
            dq_out[1][:, h * head:(h + 1) * head] = part[rows:, :]


def finish_kernel(rows, info, dq_own, dq_other, own, shared, dq, dk, dv, kept):
    head = dk.shape[1]
    dq[...] = (dq_own[...] + dq_other[...]).astype(bf16)
    dk[...] = own[0:rows, 0:head].astype(bf16)
    dv[...] = own[0:rows, head:].astype(bf16)
    kept[...] = shared[...]


def call(kernel, out_shapes, args, flops, scratch=()):
    smem, vmem = pl.BlockSpec(memory_space=pltpu.SMEM), pl.BlockSpec(memory_space=pltpu.VMEM)
    size = sum(a.size * a.dtype.itemsize for a in args)
    return pl.pallas_call(
        kernel,
        out_shape=out_shapes,
        in_specs=[smem] + [vmem] * (len(args) - 1),
        out_specs=[vmem] * len(out_shapes),
        scratch_shapes=list(scratch),
        compiler_params=pltpu.CompilerParams(vmem_limit_bytes=48 * 1024 * 1024),
        cost_estimate=pl.CostEstimate(flops=flops, bytes_accessed=size, transcendentals=0),
    )(*args)


def on_device(resp_q, resp_k, resp_v, resp_out, resp_grad, prompt_k, prompt_v, lengths):
    rows, width = resp_q.shape
    head = resp_k.shape[1]
    heads = width // head
    prompt = prompt_k.shape[0]
    c = head ** -0.5 * math.log2(math.e)
    resp_keys, prompt_keys = Z * rows, Z * prompt
    me = lax.axis_index("dev")
    info = jnp.stack([me // (Z * C), me // C % Z, me % C, lengths[0, 0]]).astype(jnp.int32)
    shape = jax.ShapeDtypeStruct

    q_other = swap_core(resp_q)
    pairs = jnp.concatenate(
        [jnp.concatenate([resp_k, resp_v], axis=1), jnp.concatenate([prompt_k, prompt_v], axis=1)], axis=0
    )
    blocks = gather(shift_z, pairs)
    column = jnp.concatenate([b[:rows] for b in blocks] + [b[rows:] for b in blocks], axis=0)
    k_all = gather(shift_x, column[:, :head])
    v_all = gather(shift_x, column[:, head:])
    grad_other = swap_core(resp_grad)

    keys = resp_keys + prompt_keys
    flops = 2 * C * rows * heads * head * keys
    st_shape = shape((3 * heads, C * rows), f32)
    st, = call(
        functools.partial(first_stats_kernel, heads, rows, c),
        [st_shape], [info, resp_q, q_other, resp_grad, resp_out, k_all[0]], flops,
    )
    st, = call(
        functools.partial(stats_kernel, heads, rows, c),
        [st_shape], [info, st, resp_q, q_other, *k_all[1:]], flops * 3,
    )
    st_other = swap_core(st)
    arrived, dq = [], []
    for i, r in enumerate((3, 1, 2, 0)):
        first, last = i == 0, i == X - 1
        out = [shape((keys, 2 * head), f32 if last else bf16)]
        out += [shape((rows, width), f32)] * 2 if last else [shape((head, C * rows * heads), f32)]
        scratch = [pltpu.VMEM((C * rows * heads, head), bf16)] * 2 + [pltpu.VMEM((keys, C * rows * heads), bf16)] * 2
        if last:
            scratch.append(pltpu.VMEM((head, C * rows * heads), f32))
        part, *dq = call(
            functools.partial(grads_kernel, heads, rows, c, STEPS[r], first, last),
            out,
            [info, st, st_other, resp_q, q_other, resp_grad, grad_other, k_all[r], v_all[r]]
            + dq + (arrived[:1] if last else []),
            5 * flops,
            scratch,
        )
        if not last:
            arrived.append(shift_x(part, -STEPS[r]))
    dq_own, dq_other = dq

    mine = (part + (arrived[1].astype(f32) + arrived[2].astype(f32))).astype(bf16)
    mine = [
        jnp.concatenate(
            [mine[r * rows:(r + 1) * rows], mine[resp_keys + r * prompt:resp_keys + (r + 1) * prompt]], axis=0
        )
        for r in range(Z)
    ]
    own = scatter_sum(shift_z, mine)
    own_prompt = own[rows:].astype(bf16)
    own_prompt = (own_prompt.astype(f32) + swap_pair(own_prompt).astype(f32)).astype(bf16)
    others = [shift_y(own_prompt, step).astype(f32) for step in (2, 1, 3)]
    grad_q, grad_k, grad_v, kept = call(
        functools.partial(finish_kernel, rows),
        [shape((rows, width), bf16)] + [shape((rows, head), bf16)] * 2 + [shape((prompt, 2 * head), bf16)],
        [info, dq_own, swap_core(dq_other), own, own_prompt],
        flops,
    )
    own_prompt = (kept.astype(f32) + others[0]) + (others[1] + others[2])
    return (grad_q, grad_k, grad_v, own_prompt[:, :head].astype(bf16), own_prompt[:, head:].astype(bf16))


def solution(mesh):
    rows, shared, group = P(("grp", "dev"), None), P("dev", None), P("grp", None)
    return jax.shard_map(
        on_device,
        mesh=mesh,
        in_specs=(rows, rows, rows, rows, rows, shared, shared, group),
        out_specs=(rows, rows, rows, shared, shared),
        check_vma=False,
    )
```

```python
import functools
import math

import jax
import jax.numpy as jnp
from jax import lax
from jax.experimental import pallas as pl
from jax.experimental.pallas import tpu as pltpu
from jax.sharding import PartitionSpec as P

X, Z, C = 4, 4, 2
STEPS = (0, 1, 3, 2)
DEV = [(x, z, c) for x in range(X) for z in range(Z) for c in range(C)]
lowest = -1e30
f32, bf16 = jnp.float32, jnp.bfloat16
NT = (((1,), (1,)), ((), ()))
NN = (((1,), (0,)), ((), ()))
TN = (((0,), (0,)), ((), ()))


def dot(a, b, dims):
    return lax.dot_general(a, b, dims, preferred_element_type=f32)


def number(x, z, c):
    return ((x % X) * Z + z % Z) * C + c % C


def swap_core(a):
    return lax.ppermute(a, "dev", [(number(x, z, c), number(x, z, c + 1)) for x, z, c in DEV])


def shift_x(a, step):
    return lax.ppermute(a, "dev", [(number(x, z, c), number(x + step, z, c)) for x, z, c in DEV])


def shift_z(a, step):
    return lax.ppermute(a, "dev", [(number(x, z, c), number(x, z + step, c)) for x, z, c in DEV])


def shift_y(a, step):
    return lax.ppermute(a, "grp", [(y * 2 + l, (y + step) % 4 * 2 + l) for y in range(4) for l in range(2)])


def swap_pair(a):
    return lax.ppermute(a, "grp", [(y * 2 + l, y * 2 + 1 - l) for y in range(4) for l in range(2)])


def gather(shift, a):
    return [a] + [shift(a, step) for step in STEPS[1:]]


def scatter_sum(shift, parts):
    total = parts[0].astype(f32)
    for step, part in zip(STEPS[1:], parts[1:]):
        total = total + shift(part, -step).astype(f32)
    return total


def row_ids(info, rows):
    place = lax.broadcasted_iota(jnp.int32, (1, C * rows), 1)
    core = jnp.where(place < rows, info[2], 1 - info[2])
    return (info[0] * Z + info[1]) * (C * rows) + core * rows + place % rows


def key_ids(info, back, rows):
    place = lax.broadcasted_iota(jnp.int32, (Z * rows, 1), 0)
    x = lax.rem(info[0] + (X - back), X)
    ids = jnp.zeros((Z * rows, 1), jnp.int32)
    for r, step in enumerate(STEPS):
        z = lax.rem(info[1] + (Z - step), Z)
        ids = jnp.where(place // rows == r, (x * Z + z) * (C * rows) + info[2] * rows + place % rows, ids)
    return ids


def seen(info, back, rows):
    x = lax.rem(info[0] + (X - back), X)
    split = info[3]
    first = x * (Z * C * rows)
    row = (info[0] * Z + info[1]) * (C * rows)
    return (x <= info[0]) & ((row < split) | (first + Z * C * rows > split))


def mask_of(info, back, rows, whole=False):
    t = row_ids(info, rows)
    u = key_ids(info, back, rows)
    mask = u >= jnp.where(t >= info[3], info[3], 0)
    return mask & (u <= t) if back == 0 or whole else mask


def masked(a, mask, fill):
    if mask is None:
        return a
    n = mask.shape[0]
    return jnp.concatenate([jnp.where(mask, a[:n], fill), a[n:]], axis=0)


def stats_step(heads, c, k, q_own, q_other, mask, st):
    head = 128
    for h in range(heads):
        cols = slice(h * head, (h + 1) * head)
        q = jnp.concatenate([q_own[:, cols], q_other[:, cols]], axis=0)
        s = masked(dot(k, q, NT) * c, mask, lowest)
        old = st[h:h + 1, :]
        new = jnp.maximum(old, jnp.max(s, axis=0, keepdims=True))
        total = jnp.sum(jnp.exp2(s - new), axis=0, keepdims=True)
        st[h:h + 1, :] = new
        st[heads + h:heads + h + 1, :] = st[heads + h:heads + h + 1, :] * jnp.exp2(old - new) + total


def first_stats_kernel(heads, rows, c, info, q_own, q_other, grad_own, out_own, k0, st):
    head = 128
    st[0:heads, :] = jnp.full((heads, C * rows), lowest, f32)
    st[heads:2 * heads, :] = jnp.zeros((heads, C * rows), f32)
    prod = grad_own[...].astype(f32) * out_own[...].astype(f32)
    for h in range(heads):
        delta = jnp.sum(prod[:, h * head:(h + 1) * head].T, axis=0, keepdims=True)
        st[2 * heads + h:2 * heads + h + 1, :] = jnp.concatenate([delta, delta], axis=1)
    stats_step(heads, c, k0[...], q_own, q_other, mask_of(info, 0, rows), st)


def stats_kernel(heads, rows, c, info, st_in, q_own, q_other, k1, k2, k3, st):
    st[...] = st_in[...]
    for k, back in zip((k1, k2, k3), STEPS[1:]):
        visible = seen(info, back, rows)

        @pl.when(visible)
        def _():
            stats_step(heads, c, k[...], q_own, q_other, mask_of(info, back, rows), st)

        @pl.when(jnp.logical_not(visible))
        def _():
            stats_step(heads, c, k[Z * rows:, :], q_own, q_other, None, st)


def combine(heads, rows, st, st_other):
    def turned(a):
        return jnp.concatenate([a[:, rows:], a[:, :rows]], axis=1)
    top, top_other = st[0:heads, :], turned(st_other[0:heads, :])
    total, total_other = st[heads:2 * heads, :], turned(st_other[heads:2 * heads, :])
    m = jnp.maximum(top, top_other)
    lse = m + jnp.log2(total * jnp.exp2(top - m) + total_other * jnp.exp2(top_other - m))
    delta = jnp.concatenate([st[2 * heads:, 0:rows], st_other[2 * heads:, 0:rows]], axis=1)
    return lse, delta


def grads_step(heads, c, k, v, q, grad, lse, delta, mask, p_all, ds_all, dq, dkv):
    head = 128
    wide = lse.shape[1]
    n = k.shape[0]
    for h in range(heads):
        at = slice(h * wide, (h + 1) * wide)
        p = masked(jnp.exp2(dot(k, q[at, :], NT) * c - lse[h:h + 1, :]), mask, 0.0)
        p_all[0:n, at] = p.astype(bf16)
        ds_all[0:n, at] = (p * (dot(v, grad[at, :], NT) - delta[h:h + 1, :])).astype(bf16)
    dq[...] += dot(k.T, ds_all[0:n, :], NN)
    dv = dot(p_all[0:n, :], grad[...], NN)
    dk = dot(ds_all[0:n, :], q[...], NN) * head ** -0.5
    return jnp.concatenate([dk, dv], axis=1)


def grads_kernel(heads, rows, c, back, first, last, info, st, st_other, q_own, q_other, grad_own, grad_other, k, v, *refs):
    head = 128
    wide = C * rows
    resp = Z * rows
    refs = list(refs)
    dq_in = None if first else refs.pop(0)
    arrived = refs.pop(0) if last else None
    dkv = refs.pop(0)
    dq_out = [refs.pop(0), refs.pop(0)] if last else [refs.pop(0)]
    q, grad, p_all, ds_all = refs[:4]
    dq = refs[4] if last else dq_out[0]
    for h in range(heads):
        cols = slice(h * head, (h + 1) * head)
        for i, (a, b) in enumerate(((q_own, grad_own), (q_other, grad_other))):
            at = slice(h * wide + i * rows, h * wide + (i + 1) * rows)
            q[at, :] = a[:, cols]
            grad[at, :] = b[:, cols]
    lse, delta = combine(heads, rows, st, st_other)
    dq[...] = jnp.zeros(dq.shape, f32) if first else dq_in[...]

    def step(a, mask):
        return grads_step(heads, c, k[a:, :], v[a:, :], q, grad, lse, delta, mask, p_all, ds_all, dq, dkv)

    if last:
        dkv[...] = arrived[...].astype(f32) + step(0, mask_of(info, back, rows))
    else:
        dkv[...] = step(0, mask_of(info, back, rows, True)).astype(bf16)
    if last:
        for h in range(heads):
            part = dq[:, h * wide:(h + 1) * wide].T * head ** -0.5
            dq_out[0][:, h * head:(h + 1) * head] = part[0:rows, :]
            dq_out[1][:, h * head:(h + 1) * head] = part[rows:, :]


def finish_kernel(rows, info, dq_own, dq_other, own, shared, dq, dk, dv, kept):
    head = dk.shape[1]
    dq[...] = (dq_own[...] + dq_other[...]).astype(bf16)
    dk[...] = own[0:rows, 0:head].astype(bf16)
    dv[...] = own[0:rows, head:].astype(bf16)
    kept[...] = shared[...]


def call(kernel, out_shapes, args, flops, scratch=()):
    smem, vmem = pl.BlockSpec(memory_space=pltpu.SMEM), pl.BlockSpec(memory_space=pltpu.VMEM)
    size = sum(a.size * a.dtype.itemsize for a in args)
    return pl.pallas_call(
        kernel,
        out_shape=out_shapes,
        in_specs=[smem] + [vmem] * (len(args) - 1),
        out_specs=[vmem] * len(out_shapes),
        scratch_shapes=list(scratch),
        compiler_params=pltpu.CompilerParams(vmem_limit_bytes=48 * 1024 * 1024),
        cost_estimate=pl.CostEstimate(flops=flops, bytes_accessed=size, transcendentals=0),
    )(*args)


def on_device(resp_q, resp_k, resp_v, resp_out, resp_grad, prompt_k, prompt_v, lengths):
    rows, width = resp_q.shape
    head = resp_k.shape[1]
    heads = width // head
    prompt = prompt_k.shape[0]
    c = head ** -0.5 * math.log2(math.e)
    resp_keys, prompt_keys = Z * rows, Z * prompt
    me = lax.axis_index("dev")
    info = jnp.stack([me // (Z * C), me // C % Z, me % C, lengths[0, 0]]).astype(jnp.int32)
    shape = jax.ShapeDtypeStruct

    q_other = swap_core(resp_q)
    pairs = jnp.concatenate(
        [jnp.concatenate([resp_k, resp_v], axis=1), jnp.concatenate([prompt_k, prompt_v], axis=1)], axis=0
    )
    blocks = gather(shift_z, pairs)
    column = jnp.concatenate([b[:rows] for b in blocks] + [b[rows:] for b in blocks], axis=0)
    k_all = gather(shift_x, column[:, :head])
    v_all = gather(shift_x, column[:, head:])
    grad_other = swap_core(resp_grad)

    keys = resp_keys + prompt_keys
    flops = 2 * C * rows * heads * head * keys
    st_shape = shape((3 * heads, C * rows), f32)
    st, = call(
        functools.partial(first_stats_kernel, heads, rows, c),
        [st_shape], [info, resp_q, q_other, resp_grad, resp_out, k_all[0]], flops,
    )
    st, = call(
        functools.partial(stats_kernel, heads, rows, c),
        [st_shape], [info, st, resp_q, q_other, *k_all[1:]], flops * 3,
    )
    st_other = swap_core(st)
    arrived, dq = [], []
    for i, r in enumerate((3, 1, 2, 0)):
        first, last = i == 0, i == X - 1
        out = [shape((keys, 2 * head), f32 if last else bf16)]
        out += [shape((rows, width), f32)] * 2 if last else [shape((head, C * rows * heads), f32)]
        scratch = [pltpu.VMEM((C * rows * heads, head), bf16)] * 2 + [pltpu.VMEM((keys, C * rows * heads), bf16)] * 2
        if last:
            scratch.append(pltpu.VMEM((head, C * rows * heads), f32))
        part, *dq = call(
            functools.partial(grads_kernel, heads, rows, c, STEPS[r], first, last),
            out,
            [info, st, st_other, resp_q, q_other, resp_grad, grad_other, k_all[r], v_all[r]]
            + dq + (arrived[:1] if last else []),
            5 * flops,
            scratch,
        )
        if not last:
            arrived.append(shift_x(part, -STEPS[r]))
    dq_own, dq_other = dq

    mine = (part + (arrived[1].astype(f32) + arrived[2].astype(f32))).astype(bf16)
    mine = [
        jnp.concatenate(
            [mine[r * rows:(r + 1) * rows], mine[resp_keys + r * prompt:resp_keys + (r + 1) * prompt]], axis=0
        )
        for r in range(Z)
    ]
    own = scatter_sum(shift_z, mine)
    own_prompt = own[rows:].astype(bf16)
    own_prompt = (own_prompt.astype(f32) + swap_pair(own_prompt).astype(f32)).astype(bf16)
    others = [shift_y(own_prompt, step).astype(f32) for step in (2, 1, 3)]
    grad_q, grad_k, grad_v, kept = call(
        functools.partial(finish_kernel, rows),
        [shape((rows, width), bf16)] + [shape((rows, head), bf16)] * 2 + [shape((prompt, 2 * head), bf16)],
        [info, dq_own, swap_core(dq_other), own, own_prompt],
        flops,
    )
    own_prompt = (kept.astype(f32) + others[0]) + (others[1] + others[2])
    return (grad_q, grad_k, grad_v, own_prompt[:, :head].astype(bf16), own_prompt[:, head:].astype(bf16))


def solution(mesh):
    rows, shared, group = P(("grp", "dev"), None), P("dev", None), P("grp", None)
    return jax.shard_map(
        on_device,
        mesh=mesh,
        in_specs=(rows, rows, rows, rows, rows, shared, shared, group),
        out_specs=(rows, rows, rows, shared, shared),
        check_vma=False,
    )
```

```python
import functools
import math

import jax
import jax.numpy as jnp
from jax import lax
from jax.experimental import pallas as pl
from jax.experimental.pallas import tpu as pltpu
from jax.sharding import PartitionSpec as P

X, Z, C = 4, 4, 2
STEPS = (0, 1, 3, 2)
DEV = [(x, z, c) for x in range(X) for z in range(Z) for c in range(C)]
lowest = -1e30
f32, bf16 = jnp.float32, jnp.bfloat16
NT = (((1,), (1,)), ((), ()))
NN = (((1,), (0,)), ((), ()))
TN = (((0,), (0,)), ((), ()))


def dot(a, b, dims):
    return lax.dot_general(a, b, dims, preferred_element_type=f32)


def number(x, z, c):
    return ((x % X) * Z + z % Z) * C + c % C


def swap_core(a):
    return lax.ppermute(a, "dev", [(number(x, z, c), number(x, z, c + 1)) for x, z, c in DEV])


def shift_x(a, step):
    return lax.ppermute(a, "dev", [(number(x, z, c), number(x + step, z, c)) for x, z, c in DEV])


def shift_z(a, step):
    return lax.ppermute(a, "dev", [(number(x, z, c), number(x, z + step, c)) for x, z, c in DEV])


def trade_y(a, bits):
    return lax.ppermute(a, "grp", [(y * 2 + l, (y ^ bits) * 2 + l) for y in range(4) for l in range(2)])


def swap_pair(a):
    return lax.ppermute(a, "grp", [(y * 2 + l, y * 2 + 1 - l) for y in range(4) for l in range(2)])


def gather(shift, a):
    return [a] + [shift(a, step) for step in STEPS[1:]]


def scatter_sum(shift, parts):
    total = parts[0].astype(f32)
    for step, part in zip(STEPS[1:], parts[1:]):
        total = total + shift(part, -step).astype(f32)
    return total


def row_ids(info, rows):
    place = lax.broadcasted_iota(jnp.int32, (1, C * rows), 1)
    core = jnp.where(place < rows, info[2], 1 - info[2])
    return (info[0] * Z + info[1]) * (C * rows) + core * rows + place % rows


def key_ids(info, back, rows):
    place = lax.broadcasted_iota(jnp.int32, (Z * rows, 1), 0)
    x = lax.rem(info[0] + (X - back), X)
    ids = jnp.zeros((Z * rows, 1), jnp.int32)
    for r, step in enumerate(STEPS):
        z = lax.rem(info[1] + (Z - step), Z)
        ids = jnp.where(place // rows == r, (x * Z + z) * (C * rows) + info[2] * rows + place % rows, ids)
    return ids


def seen(info, back, rows):
    x = lax.rem(info[0] + (X - back), X)
    split = info[3]
    first = x * (Z * C * rows)
    row = (info[0] * Z + info[1]) * (C * rows)
    return (x <= info[0]) & ((row < split) | (first + Z * C * rows > split))


def mask_of(info, back, rows):
    t = row_ids(info, rows)
    u = key_ids(info, back, rows)
    mask = u >= jnp.where(t >= info[3], info[3], 0)
    return mask & (u <= t) if back == 0 else mask


def masked(a, mask, fill):
    if mask is None:
        return a
    n = mask.shape[0]
    return jnp.concatenate([jnp.where(mask, a[:n], fill), a[n:]], axis=0)


def stats_step(heads, c, k, q_own, q_other, mask, st):
    head = 128
    for h in range(heads):
        cols = slice(h * head, (h + 1) * head)
        q = jnp.concatenate([q_own[:, cols], q_other[:, cols]], axis=0)
        s = masked(dot(k, q, NT) * c, mask, lowest)
        old = st[h:h + 1, :]
        new = jnp.maximum(old, jnp.max(s, axis=0, keepdims=True))
        total = jnp.sum(jnp.exp2(s - new), axis=0, keepdims=True)
        st[h:h + 1, :] = new
        st[heads + h:heads + h + 1, :] = st[heads + h:heads + h + 1, :] * jnp.exp2(old - new) + total


def first_stats_kernel(heads, rows, c, info, q_own, q_other, grad_own, out_own, k0, st):
    head = 128
    st[0:heads, :] = jnp.full((heads, C * rows), lowest, f32)
    st[heads:2 * heads, :] = jnp.zeros((heads, C * rows), f32)
    prod = grad_own[...].astype(f32) * out_own[...].astype(f32)
    for h in range(heads):
        delta = jnp.sum(prod[:, h * head:(h + 1) * head].T, axis=0, keepdims=True)
        st[2 * heads + h:2 * heads + h + 1, :] = jnp.concatenate([delta, delta], axis=1)
    stats_step(heads, c, k0[...], q_own, q_other, mask_of(info, 0, rows), st)


def stats_kernel(heads, rows, c, info, st_in, q_own, q_other, k1, k2, k3, st):
    st[...] = st_in[...]
    for k, back in zip((k1, k2, k3), STEPS[1:]):
        visible = seen(info, back, rows)

        @pl.when(visible)
        def _():
            stats_step(heads, c, k[...], q_own, q_other, mask_of(info, back, rows), st)

        @pl.when(jnp.logical_not(visible))
        def _():
            stats_step(heads, c, k[Z * rows:, :], q_own, q_other, None, st)


def combine(heads, rows, st, st_other):
    def turned(a):
        return jnp.concatenate([a[:, rows:], a[:, :rows]], axis=1)
    top, top_other = st[0:heads, :], turned(st_other[0:heads, :])
    total, total_other = st[heads:2 * heads, :], turned(st_other[heads:2 * heads, :])
    m = jnp.maximum(top, top_other)
    lse = m + jnp.log2(total * jnp.exp2(top - m) + total_other * jnp.exp2(top_other - m))
    delta = jnp.concatenate([st[2 * heads:, 0:rows], st_other[2 * heads:, 0:rows]], axis=1)
    return lse, delta


def grads_step(heads, c, k, v, q, grad, lse, delta, mask, p_all, ds_all, dq, dkv):
    head = 128
    wide = lse.shape[1]
    n = k.shape[0]
    for h in range(heads):
        at = slice(h * wide, (h + 1) * wide)
        p = masked(jnp.exp2(dot(k, q[at, :], NT) * c - lse[h:h + 1, :]), mask, 0.0)
        p_all[0:n, at] = p.astype(bf16)
        ds_all[0:n, at] = (p * (dot(v, grad[at, :], NT) - delta[h:h + 1, :])).astype(bf16)
    dq[...] += dot(k.T, ds_all[0:n, :], NN)
    dv = dot(p_all[0:n, :], grad[...], NN)
    dk = dot(ds_all[0:n, :], q[...], NN) * head ** -0.5
    return jnp.concatenate([dk, dv], axis=1)


def grads_kernel(heads, rows, c, back, first, last, info, st, st_other, q_own, q_other, grad_own, grad_other, k, v, *refs):
    head = 128
    wide = C * rows
    resp = Z * rows
    refs = list(refs)
    dq_in = None if first else refs.pop(0)
    arrived = refs.pop(0) if last else None
    dkv = refs.pop(0)
    dq_out = [refs.pop(0), refs.pop(0)] if last else [refs.pop(0)]
    q, grad, p_all, ds_all = refs[:4]
    dq = refs[4] if last else dq_out[0]
    for h in range(heads):
        cols = slice(h * head, (h + 1) * head)
        for i, (a, b) in enumerate(((q_own, grad_own), (q_other, grad_other))):
            at = slice(h * wide + i * rows, h * wide + (i + 1) * rows)
            q[at, :] = a[:, cols]
            grad[at, :] = b[:, cols]
    lse, delta = combine(heads, rows, st, st_other)
    dq[...] = jnp.zeros(dq.shape, f32) if first else dq_in[...]

    def step(a, mask):
        return grads_step(heads, c, k[a:, :], v[a:, :], q, grad, lse, delta, mask, p_all, ds_all, dq, dkv)

    if back == 0:
        dkv[...] = arrived[...].astype(f32) + step(0, mask_of(info, back, rows))
    else:
        visible = seen(info, back, rows)

        @pl.when(visible)
        def _():
            dkv[...] = step(0, mask_of(info, back, rows)).astype(bf16)

        @pl.when(jnp.logical_not(visible))
        def _():
            dkv[0:resp, :] = jnp.zeros((resp, 2 * head), bf16)
            dkv[resp:, :] = step(resp, None).astype(bf16)
    if last:
        for h in range(heads):
            part = dq[:, h * wide:(h + 1) * wide].T * head ** -0.5
            dq_out[0][:, h * head:(h + 1) * head] = part[0:rows, :]
            dq_out[1][:, h * head:(h + 1) * head] = part[rows:, :].astype(bf16)


def finish_kernel(rows, info, dq_own, dq_other, own, shared, dq, dk, dv, kept):
    head = dk.shape[1]
    dq[...] = (dq_own[...] + dq_other[...].astype(f32)).astype(bf16)
    dk[...] = own[0:rows, 0:head].astype(bf16)
    dv[...] = own[0:rows, head:].astype(bf16)
    kept[...] = shared[...]


def call(kernel, out_shapes, args, flops, scratch=()):
    smem, vmem = pl.BlockSpec(memory_space=pltpu.SMEM), pl.BlockSpec(memory_space=pltpu.VMEM)
    size = sum(a.size * a.dtype.itemsize for a in args)
    return pl.pallas_call(
        kernel,
        out_shape=out_shapes,
        in_specs=[smem] + [vmem] * (len(args) - 1),
        out_specs=[vmem] * len(out_shapes),
        scratch_shapes=list(scratch),
        compiler_params=pltpu.CompilerParams(vmem_limit_bytes=48 * 1024 * 1024),
        cost_estimate=pl.CostEstimate(flops=flops, bytes_accessed=size, transcendentals=0),
    )(*args)


def on_device(resp_q, resp_k, resp_v, resp_out, resp_grad, prompt_k, prompt_v, lengths):
    rows, width = resp_q.shape
    head = resp_k.shape[1]
    heads = width // head
    prompt = prompt_k.shape[0]
    c = head ** -0.5 * math.log2(math.e)
    resp_keys, prompt_keys = Z * rows, Z * prompt
    me = lax.axis_index("dev")
    info = jnp.stack([me // (Z * C), me // C % Z, me % C, lengths[0, 0]]).astype(jnp.int32)
    shape = jax.ShapeDtypeStruct

    q_other = swap_core(resp_q)
    pairs = jnp.concatenate(
        [jnp.concatenate([resp_k, resp_v], axis=1), jnp.concatenate([prompt_k, prompt_v], axis=1)], axis=0
    )
    blocks = gather(shift_z, pairs)
    column = jnp.concatenate([b[:rows] for b in blocks] + [b[rows:] for b in blocks], axis=0)
    k_all = gather(shift_x, column[:, :head])
    v_all = gather(shift_x, column[:, head:])
    grad_other = swap_core(resp_grad)

    keys = resp_keys + prompt_keys
    flops = 2 * C * rows * heads * head * keys
    st_shape = shape((3 * heads, C * rows), f32)
    st, = call(
        functools.partial(first_stats_kernel, heads, rows, c),
        [st_shape], [info, resp_q, q_other, resp_grad, resp_out, k_all[0]], flops,
    )
    st, = call(
        functools.partial(stats_kernel, heads, rows, c),
        [st_shape], [info, st, resp_q, q_other, *k_all[1:]], flops * 3,
    )
    st_other = swap_core(st)
    arrived, dq = [], []
    for i, r in enumerate((3, 1, 2, 0)):
        first, last = i == 0, i == X - 1
        out = [shape((keys, 2 * head), f32 if last else bf16)]
        out += [shape((rows, width), f32), shape((rows, width), bf16)] if last else [shape((head, C * rows * heads), f32)]
        scratch = [pltpu.VMEM((C * rows * heads, head), bf16)] * 2 + [pltpu.VMEM((keys, C * rows * heads), bf16)] * 2
        if last:
            scratch.append(pltpu.VMEM((head, C * rows * heads), f32))
        part, *dq = call(
            functools.partial(grads_kernel, heads, rows, c, STEPS[r], first, last),
            out,
            [info, st, st_other, resp_q, q_other, resp_grad, grad_other, k_all[r], v_all[r]]
            + dq + (arrived[:1] if last else []),
            5 * flops,
            scratch,
        )
        if not last:
            arrived.append(shift_x(part, -STEPS[r]))
    dq_own, dq_other = dq

    mine = (part + (arrived[1].astype(f32) + arrived[2].astype(f32))).astype(bf16)
    mine = [
        jnp.concatenate(
            [mine[r * rows:(r + 1) * rows], mine[resp_keys + r * prompt:resp_keys + (r + 1) * prompt]], axis=0
        )
        for r in range(Z)
    ]
    own = scatter_sum(shift_z, mine)
    own_prompt = own[rows:].astype(bf16)
    own_prompt = (own_prompt.astype(f32) + swap_pair(own_prompt).astype(f32)).astype(bf16)
    own_prompt = (own_prompt.astype(f32) + trade_y(own_prompt, 1).astype(f32)).astype(bf16)
    other = trade_y(own_prompt, 2).astype(f32)
    grad_q, grad_k, grad_v, kept = call(
        functools.partial(finish_kernel, rows),
        [shape((rows, width), bf16)] + [shape((rows, head), bf16)] * 2 + [shape((prompt, 2 * head), bf16)],
        [info, dq_own, swap_core(dq_other), own, own_prompt],
        flops,
    )
    own_prompt = kept.astype(f32) + other
    return (grad_q, grad_k, grad_v, own_prompt[:, :head].astype(bf16), own_prompt[:, head:].astype(bf16))


def solution(mesh):
    rows, shared, group = P(("grp", "dev"), None), P("dev", None), P("grp", None)
    return jax.shard_map(
        on_device,
        mesh=mesh,
        in_specs=(rows, rows, rows, rows, rows, shared, shared, group),
        out_specs=(rows, rows, rows, shared, shared),
        check_vma=False,
    )
```
